32 devices in a mesh: sx: 4 (over y, x), sy: 4 (over z), grp: 2 (over core).
Axes of the slice: x: 2, y: 2, z: 4, core: 2. Of those that a mesh axis runs over, the one named last changes fastest.
Arguments:
- impedance: bfloat16 [4, 4, 6144, 6144], P('sx', 'sy', 'grp'), may hold values from -0.078125 to 0.078125
- sources: bfloat16 [4, 4, 6144, 128], P('sx', 'sy', 'grp'), may hold values from -6 to 6
- match: int32 [4, 4, 6144], P('sx', 'sy'), may hold values from 0 to 6143, as said below
Outputs:
- traces: bfloat16 [4, 4, 6144, 128], P('sx', 'sy', 'grp')
The draws below stay inside these ranges and needn't reach their ends.
Inputs may be any that keep to these rules, and one draw needn't show every extreme that they name: For every subdomain, match maps the first 3072 positions onto a permutation of 0 to 3071 and the last 3072 positions onto a permutation of 3072 to 6143.
All inputs are finite; a program needn't handle non-finite values.
Results may differ from the reference program's by a relative error of at most 0.0085.
Values may be sent and summed in bfloat16 or wider, within the bound.
No kernel may reach another device: no remote copies, remote signals or barrier semaphores. Data moves between devices by JAX's collectives and lax.ppermute only.
A program may use at most 192 MiB of HBM per device.

```python
import jax
import jax.numpy as jnp
from jax import lax

M = 6144
SRC = 128
N_SX = 4
N_SY = 4


def draw_match(key, part):
    count = N_SX * N_SY * 2
    keys = jax.random.split(jax.random.fold_in(key, 17), count)
    perms = jax.vmap(lambda k: jax.random.permutation(k, M // 2))(keys)
    perms = perms.reshape(N_SX, N_SY, 2, M // 2).astype(jnp.int32)
    offset = jnp.array([0, M // 2], jnp.int32).reshape(1, 1, 2, 1)
    return (perms + offset).reshape(N_SX, N_SY, M)


def shard_levels(own_key, shape, shards, low, largest):
    level = 1.0
    for position, parts in shards:
        heights = jax.random.uniform(jax.random.fold_in(jax.random.fold_in(own_key, 6), position), (parts,), jnp.float32, low / len(shards), largest / len(shards))
        level = level * jnp.repeat(jnp.exp(heights), shape[position] // parts).reshape((-1,) + (1,) * (len(shape) - 1 - position))
    return level


def centred(rng, extent, width, reach, pieces=(), kind=jnp.bfloat16):
    drawn = jax.random.normal(rng, extent, jnp.float32) * width
    if len(pieces) > 0:
        drawn = shard_levels(rng, extent, pieces, -0.22, 0.18) * drawn
    return jnp.clip(drawn, min=-reach, max=reach).astype(kind)


def setup_inputs(seed: int = 0) -> dict:
    key_list = jax.random.split(jax.random.key(seed), 4)
    return {
        "impedance": centred(key_list[0], (N_SX, N_SY, M, M), M ** -0.5, 0.078125, ((0, 4), (1, 4), (2, 2))),
        "sources": centred(key_list[1], (N_SX, N_SY, M, SRC), 1.0, 6.0, ((0, 4), (1, 4), (2, 2))),
        "match": draw_match(jax.random.fold_in(key_list[3], 71), 0),
    }


def reference(impedance, sources, match):
    half = M // 2
    zero_half = jnp.zeros((half, SRC), jnp.bfloat16)
    done = {}
    for diag in range(N_SX + N_SY - 1):
        for col in range(N_SX):
            row = diag - col
            if row < 0 or row >= N_SY:
                continue
            west = done[(col - 1, row)][:half] if col > 0 else zero_half
            south = done[(col, row - 1)][half:] if row > 0 else zero_half
            gathered = jnp.concatenate([west, south], axis=0)
            incoming = jnp.take(gathered, match[col, row].astype(jnp.int32), axis=0)
            product = jnp.dot(impedance[col, row].astype(jnp.float32), incoming.astype(jnp.float32),
                              precision=lax.Precision.HIGHEST, preferred_element_type=jnp.float32)
            done[(col, row)] = (product + sources[col, row].astype(jnp.float32)).astype(jnp.bfloat16)
    rows_out = []
    for col in range(N_SX):
        rows_out.append(jnp.stack([done[(col, row)] for row in range(N_SY)], axis=0))
    return jnp.stack(rows_out, axis=0)
```

```python
import functools

import jax
import jax.numpy as jnp
from jax import lax
from jax.experimental import pallas as pl
from jax.experimental.pallas import tpu as pltpu
from jax.sharding import PartitionSpec as P

AXES = ("sx", "sy", "grp")
IN_VMEM = pl.BlockSpec(memory_space=pltpu.VMEM)
IN_SMEM = pl.BlockSpec(memory_space=pltpu.SMEM)
PARAMS = pltpu.CompilerParams(vmem_limit_bytes=6 * 2**20)
PARTS = 4


def from_behind(block, axis, distance):
    devices = range(lax.axis_size(axis))
    route = [(i - distance, i) for i in devices if i - distance in devices]
    return lax.ppermute(block, axis, route)


def any_group(impedance, sources, match):
    zmatrix = impedance[0, 0]
    local_src = sources[0, 0].astype(jnp.float32)
    order = match[0, 0]
    total = zmatrix.shape[1]
    half = total // 2
    inverse = jnp.argsort(order)
    folded = jnp.take(zmatrix, inverse, axis=1)
    west_map = folded[:, :half]
    south_map = folded[:, half:]
    sweeps = lax.axis_size("sx") + lax.axis_size("sy") - 1
    outgoing = jnp.zeros(sources.shape[2:], jnp.bfloat16)
    for sweep_step in range(sweeps):
        whole = lax.all_gather(outgoing, "grp", axis=0, tiled=True)
        from_west = from_behind(whole[:half], "sx", 1)
        from_south = from_behind(whole[half:], "sy", 1)
        product = jnp.dot(west_map, from_west, preferred_element_type=jnp.float32)
        product = product + jnp.dot(south_map, from_south, preferred_element_type=jnp.float32)
        outgoing = (product + local_src).astype(jnp.bfloat16)
    return outgoing[None, None]


def routes(n_sx, n_sy, diagonal=None):
    number = lambda i, j, g: (i * n_sy + j) * 2 + g
    pairs = []
    for i in range(n_sx):
        for j in range(n_sy):
            if diagonal is not None and i + j != diagonal:
                continue
            if i + 1 < n_sx:
                pairs.append((number(i, j, 0), number(i + 1, j, 0)))
            if j + 1 < n_sy:
                pairs.append((number(i, j, 1), number(i, j + 1, 1)))
    return pairs


def is_active(step):
    diagonal = lax.axis_index("sx") + lax.axis_index("sy")
    if step == 0:
        return diagonal == 0
    if step == 1:
        return diagonal <= 1
    return diagonal == step


def row_block(rows):
    return next(b for b in (512, 256, 128, 64, 32, 16, rows) if rows % b == 0)


def multiply(pieces, acc):
    rows = acc.shape[0]
    block = row_block(rows)
    for b in range(0, rows, block):
        total = acc[b:b + block, :]
        for slab, trace in pieces:
            total = total + jnp.dot(slab[b:b + block, :], trace[...], preferred_element_type=jnp.float32)
        acc[b:b + block, :] = total


def pick_rows(order, acc, out):
    count = out.shape[0]
    some = next(b for b in (64, 32, 16, count) if count % b == 0)

    @pl.loop(0, count // some)
    def _(t):
        first = pl.multiple_of(t * some, some)
        rows = [acc[pl.ds(order[first + u], 1), :] for u in range(some)]
        out[pl.ds(first, some), :] = jnp.concatenate(rows, axis=0).astype(out.dtype)


def multiply_kernel(step, count, *refs):
    pieces = [(refs[2 * n], refs[2 * n + 1]) for n in range(count)]
    refs = refs[2 * count:]
    acc = refs[-1] if len(refs) == 2 else refs[-2]

    @pl.when(is_active(step))
    def _():
        multiply(pieces, acc)
        if len(refs) == 4:
            pick_rows(refs[0], acc, refs[3])


def pick_kernel(step, order, acc, out):
    @pl.when(is_active(step))
    def _():
        pick_rows(order, acc, out)


def multiply_call(step, pieces, order, acc):
    args, specs = [], []
    for piece in pieces:
        args += [pltpu.with_memory_space_constraint(piece[0], pltpu.VMEM), piece[1]]
        specs += [IN_VMEM, IN_VMEM]
    if order is not None:
        args.append(order)
        specs.append(IN_SMEM)
    args.append(pltpu.with_memory_space_constraint(acc, pltpu.VMEM))
    specs.append(IN_VMEM)
    shapes, outs = [pltpu.VMEM(acc.shape, acc.dtype)], [IN_VMEM]
    if order is not None:
        shapes.append(jax.ShapeDtypeStruct((order.shape[0], acc.shape[1]), jnp.bfloat16))
        outs.append(IN_VMEM)
    return pl.pallas_call(
        functools.partial(multiply_kernel, step, len(pieces)),
        out_shape=tuple(shapes), in_specs=specs, out_specs=tuple(outs),
        input_output_aliases={len(args) - 1: 0}, compiler_params=PARAMS,
    )(*args)


def pick_call(step, order, acc):
    return pl.pallas_call(
        functools.partial(pick_kernel, step),
        out_shape=jax.ShapeDtypeStruct((order.shape[0], acc.shape[1]), jnp.bfloat16),
        in_specs=[IN_SMEM, IN_VMEM], out_specs=IN_VMEM, compiler_params=PARAMS,
    )(order, pltpu.with_memory_space_constraint(acc, pltpu.VMEM))


def load_kernel(size, zmap, *refs):
    slabs, arrived = refs[:-1], refs[-1]
    half = zmap.shape[1] // 2
    core = lax.axis_index("grp")
    copies = []
    for n, slab in enumerate(slabs):
        side, c = ((core, n) if n < PARTS else (1 - core, n - PARTS))
        start = pl.multiple_of(side * half + c * size, 128)
        copies.append(pltpu.make_async_copy(zmap.at[:, pl.ds(start, size)], slab, arrived.at[n]))
    for copy in copies:
        copy.start()
    for copy in copies:
        copy.wait()


def load_call(zmap, size):
    count = 2 * PARTS
    return pl.pallas_call(
        functools.partial(load_kernel, size),
        out_shape=tuple([pltpu.VMEM((zmap.shape[0], size), zmap.dtype)] * count),
        in_specs=[pl.BlockSpec(memory_space=pl.ANY)], out_specs=tuple([IN_VMEM] * count),
        scratch_shapes=[pltpu.SemaphoreType.DMA((count,))], compiler_params=PARAMS,
    )(zmap)


def core_pair(impedance, sources, match):
    n_sx, n_sy = lax.axis_size("sx"), lax.axis_size("sy")
    core = lax.axis_index("grp")
    half = impedance.shape[3] // 2
    size = half // PARTS
    starts = [size * c for c in range(PARTS)]

    wanted = lax.dynamic_slice(match[0, 0], (core * half,), (half,)) - core * half
    back = [(b, a) for a, b in routes(n_sx, n_sy)]
    order = lax.ppermute(wanted, AXES, back)
    orders = [order[at:at + size] for at in starts]

    acc = sources[0, 0].astype(jnp.float32)
    sends = [pick_call(0, o, acc) for o in orders]
    zmap, sends = lax.optimization_barrier((impedance[0, 0], sends))
    slabs = load_call(zmap, size)
    steps = n_sx + n_sy - 2
    for step in range(1, steps + 1):
        pairs = routes(n_sx, n_sy, step - 1)
        owns = [lax.ppermute(s, AXES, pairs) for s in sends]
        pending = []
        for c, own in enumerate(owns):
            if c:
                acc, own = lax.optimization_barrier((acc, own))
            swapped = lax.ppermute(own, "grp", [(0, 1), (1, 0)])
            acc, = multiply_call(step, [(slabs[c], own)] + pending, None, acc)
            pending = [(slabs[PARTS + c], swapped)]
        if step == steps:
            acc, = multiply_call(step, pending, None, acc)
        else:
            acc, first = multiply_call(step, pending, orders[0], acc)
            sends = [first] + [pick_call(step, o, acc) for o in orders[1:]]
    return acc.astype(jnp.bfloat16)[None, None]


def solution(mesh):
    placed = (P("sx", "sy", "grp", None), P("sx", "sy", "grp", None), P("sx", "sy", None))
    body = core_pair if mesh.shape["grp"] == 2 else any_group
    return jax.shard_map(
        body, mesh=mesh, in_specs=placed, out_specs=P("sx", "sy", "grp", None), check_vma=False
    )
```

```python
import functools

import jax
import jax.numpy as jnp
from jax import lax
from jax.experimental import pallas as pl
from jax.experimental.pallas import tpu as pltpu
from jax.sharding import PartitionSpec as P

AXES = ("sx", "sy", "grp")
IN_VMEM = pl.BlockSpec(memory_space=pltpu.VMEM)
IN_PLACE = pl.BlockSpec(memory_space=pl.ANY)
PARAMS = pltpu.CompilerParams(vmem_limit_bytes=6 * 2**20)
LOADING = pltpu.CompilerParams(vmem_limit_bytes=9 * 2**20)
SHORT = pl.CostEstimate(flops=1, bytes_accessed=1, transcendentals=0)
LATE = 1
STAGES = 4
SHARES = (8, 8, 8)


def from_behind(block, axis, distance):
    devices = range(lax.axis_size(axis))
    route = [(i - distance, i) for i in devices if i - distance in devices]
    return lax.ppermute(block, axis, route)


def any_group(impedance, sources, match):
    zmatrix = impedance[0, 0]
    local_src = sources[0, 0].astype(jnp.float32)
    order = match[0, 0]
    total = zmatrix.shape[1]
    half = total // 2
    inverse = jnp.argsort(order)
    folded = jnp.take(zmatrix, inverse, axis=1)
    west_map = folded[:, :half]
    south_map = folded[:, half:]
    sweeps = lax.axis_size("sx") + lax.axis_size("sy") - 1
    outgoing = jnp.zeros(sources.shape[2:], jnp.bfloat16)
    for sweep_step in range(sweeps):
        whole = lax.all_gather(outgoing, "grp", axis=0, tiled=True)
        from_west = from_behind(whole[:half], "sx", 1)
        from_south = from_behind(whole[half:], "sy", 1)
        product = jnp.dot(west_map, from_west, preferred_element_type=jnp.float32)
        product = product + jnp.dot(south_map, from_south, preferred_element_type=jnp.float32)
        outgoing = (product + local_src).astype(jnp.bfloat16)
    return outgoing[None, None]


def routes(n_sx, n_sy, diagonal=None):
    number = lambda i, j, g: (i * n_sy + j) * 2 + g
    pairs = []
    for i in range(n_sx):
        for j in range(n_sy):
            if diagonal is not None and i + j != diagonal:
                continue
            if i + 1 < n_sx:
                pairs.append((number(i, j, 0), number(i + 1, j, 0)))
            if j + 1 < n_sy:
                pairs.append((number(i, j, 1), number(i, j + 1, 1)))
    return pairs


def is_active(step):
    diagonal = lax.axis_index("sx") + lax.axis_index("sy")
    if step == LATE:
        return (diagonal == step) | (diagonal == 0)
    return diagonal == step


def spans(half):
    unit = half // sum(SHARES)
    if half % sum(SHARES) or unit % 128:
        return [(0, half)]
    starts = [unit * sum(SHARES[:c]) for c in range(len(SHARES))]
    return [(at, unit * share) for at, share in zip(starts, SHARES)]


def block_of(extent, largest=512):
    return next(b for b in (largest, 256, 128, extent) if extent % b == 0)


def held(array):
    return pltpu.with_memory_space_constraint(array, pltpu.VMEM)


def load_kernel(pieces, zmap, *refs):
    stage, arrived = refs[-2:]
    slabs = refs[-2 - len(pieces):-2]
    depth, block, half = stage.shape
    count = zmap.shape[0] // block
    core = lax.axis_index("grp")

    side = core if pieces[0][0] else 1 - core

    def fetch(n):
        start = pl.multiple_of(side * half, 128)
        return pltpu.make_async_copy(
            zmap.at[pl.ds(n * block, block), pl.ds(start, half)], stage.at[n % depth], arrived.at[n % depth])

    for n in range(min(depth - 1, count)):
        fetch(n).start()
    for n in range(count):
        if n + depth - 1 < count:
            fetch(n + depth - 1).start()
        fetch(n).wait()
        for slab, (_, at, size) in zip(slabs, pieces):
            width = block_of(size, 256)
            for k in range(0, size, width):
                slab[k:k + width, n * block:(n + 1) * block] = stage[n % depth, :, at + k:at + k + width].T


def load_call(zmap, pieces):
    rows, half = zmap.shape[0], zmap.shape[1] // 2
    return pl.pallas_call(
        functools.partial(load_kernel, pieces),
        out_shape=tuple(pltpu.VMEM((size, rows), zmap.dtype) for _, _, size in pieces),
        in_specs=[IN_PLACE], out_specs=tuple([IN_VMEM] * len(pieces)),
        scratch_shapes=[pltpu.VMEM((STAGES, block_of(rows, 256), half), zmap.dtype), pltpu.SemaphoreType.DMA((STAGES,))],
        compiler_params=LOADING, cost_estimate=pl.CostEstimate(
            flops=0, bytes_accessed=2 * rows * half, transcendentals=0),
    )(zmap)


def add_products(pieces, old, new):
    extent = new.shape[1]
    block = block_of(extent, 1024)
    flat = [(slab, trace[...].T) for slab, trace in pieces]
    for b in range(0, extent, block):
        total = None if old is None else old[:, b:b + block]
        for slab, trace in flat:
            term = jnp.dot(trace, slab[:, b:b + block], preferred_element_type=jnp.float32)
            total = term if total is None else total + term
        new[:, b:b + block] = total


def pick_rows(order, rows, out):
    count = out.shape[0]
    some = next(b for b in (64, 32, 16, count) if count % b == 0)

    @pl.loop(0, count // some)
    def _(t):
        first = pl.multiple_of(t * some, some)
        picked = [rows[pl.ds(order[first + u], 1), :] for u in range(some)]
        out[pl.ds(first, some), :] = jnp.concatenate(picked, axis=0).astype(out.dtype)


def multiply_kernel(step, count, *refs):
    pieces = [(refs[2 * n], refs[2 * n + 1]) for n in range(count)]
    refs = refs[2 * count:]

    @pl.when(is_active(step))
    def _():
        add_products(pieces, refs[0] if len(refs) == 2 else None, refs[-1])


def finish_kernel(step, picks, slab, trace, acc, sources, *refs):
    if picks:
        order, _, rows, out, places, arrived = refs
        fetch = pltpu.make_async_copy(order, places, arrived)
    else:
        _, rows, out = refs

    @pl.when(is_active(step))
    def _():
        if picks:
            fetch.start()
        flat = trace[...].T
        extent = acc.shape[1]
        block = block_of(extent, 512)
        for b in range(0, extent, block):
            total = acc[:, b:b + block] + jnp.dot(
                flat, slab[:, b:b + block], preferred_element_type=jnp.float32)
            rows[b:b + block, :] = total.T + sources[b:b + block, :].astype(jnp.float32)
        if picks:
            fetch.wait()
            pick_rows(places, rows, out)

    if not picks:
        out[...] = rows[...].astype(out.dtype)


def pick_kernel(step, order, rows, out, places, arrived):
    @pl.when(is_active(step))
    def _():
        fetch = pltpu.make_async_copy(order, places, arrived)
        fetch.start()
        fetch.wait()
        pick_rows(places, rows, out)


def multiply_call(step, pieces, acc, rows, columns):
    args = [a for slab, trace in pieces for a in (held(slab), trace)]
    if acc is not None:
        args.append(held(acc))
    return pl.pallas_call(
        functools.partial(multiply_kernel, step, len(pieces)),
        out_shape=pltpu.VMEM((columns, rows), jnp.float32), in_specs=[IN_VMEM] * len(args), out_specs=IN_VMEM,
        input_output_aliases={} if acc is None else {len(args) - 1: 0}, compiler_params=PARAMS, cost_estimate=SHORT,
    )(*args)


def places_for(order):
    return [pltpu.SMEM(order.shape, order.dtype), pltpu.SemaphoreType.DMA]


def finish_call(step, slab, trace, acc, sources, order, rows):
    args = [held(slab), trace, held(acc), held(sources)]
    specs = [IN_VMEM] * 4
    if order is not None:
        args.append(order)
        specs.append(IN_PLACE)
        out = pltpu.VMEM((order.shape[0], rows.shape[1]), jnp.bfloat16)
    else:
        out = jax.ShapeDtypeStruct(rows.shape, jnp.bfloat16)
    args.append(held(rows))
    specs.append(IN_VMEM)
    return pl.pallas_call(
        functools.partial(finish_kernel, step, order is not None),
        out_shape=(pltpu.VMEM(rows.shape, rows.dtype), out), in_specs=specs, out_specs=(IN_VMEM, IN_VMEM),
        scratch_shapes=[] if order is None else places_for(order),
        input_output_aliases={len(args) - 1: 0}, compiler_params=PARAMS, cost_estimate=SHORT,
    )(*args)


def pick_call(step, order, rows):
    return pl.pallas_call(
        functools.partial(pick_kernel, step),
        out_shape=pltpu.VMEM((order.shape[0], rows.shape[1]), jnp.bfloat16),
        in_specs=[IN_PLACE, IN_VMEM], out_specs=IN_VMEM, scratch_shapes=places_for(order),
        compiler_params=PARAMS, cost_estimate=SHORT,
    )(order, held(rows))


def widen_kernel(source, rows):
    rows[...] = source[...].astype(rows.dtype)


def widen_call(source):
    return pl.pallas_call(
        widen_kernel, out_shape=pltpu.VMEM(source.shape, jnp.float32), in_specs=[IN_VMEM], out_specs=IN_VMEM,
        compiler_params=PARAMS, cost_estimate=SHORT,
    )(held(source))


def core_pair(impedance, sources, match):
    n_sx, n_sy = lax.axis_size("sx"), lax.axis_size("sy")
    core = lax.axis_index("grp")
    half = impedance.shape[3] // 2
    height, columns = sources.shape[2:]
    parts = spans(half)
    count = len(parts)
    source = sources[0, 0]

    wanted = lax.dynamic_slice(match[0, 0], (core * half,), (half,)) - core * half
    back = [(b, a) for a, b in routes(n_sx, n_sy)]
    order = lax.ppermute(wanted, AXES, back)
    orders = [order[at:at + size] for at, size in parts]

    zmap = impedance[0, 0]
    near = [(True, at, size) for at, size in parts]
    far = [(False, at, size) for at, size in parts]
    slabs = list(load_call(zmap, near))
    slabs, source = lax.optimization_barrier((slabs, source))
    rows = widen_call(source)
    sends = [pick_call(0, order, rows) for order in orders]
    zmap, sends = lax.optimization_barrier((zmap, sends))
    slabs = lax.optimization_barrier((*slabs, *load_call(zmap, far)))
    steps = n_sx + n_sy - 2
    for step in range(1, steps + 1):
        pairs = routes(n_sx, n_sy, step - 1)
        owns = [lax.ppermute(s, AXES, pairs) for s in sends]
        acc, waiting = None, []
        for c, own in enumerate(owns):
            if c:
                acc, own = lax.optimization_barrier((acc, own))
            pieces = [(slabs[c], own)]
            if c + 1 == count:
                pieces, waiting = pieces + waiting, []
            waiting.append((slabs[count + c], lax.ppermute(own, "grp", [(0, 1), (1, 0)])))
            acc = multiply_call(step, pieces, acc, height, columns)
        (slab, trace), = waiting
        if step == steps:
            rows, traces = finish_call(step, slab, trace, acc, source, None, rows)
        else:
            rows, first = finish_call(step, slab, trace, acc, source, orders[0], rows)
            sends = [first] + [pick_call(step, order, rows) for order in orders[1:]]
    return traces[None, None]


def solution(mesh):
    placed = (P("sx", "sy", "grp", None), P("sx", "sy", "grp", None), P("sx", "sy", None))
    body = core_pair if mesh.shape["grp"] == 2 else any_group
    return jax.shard_map(
        body, mesh=mesh, in_specs=placed, out_specs=P("sx", "sy", "grp", None), check_vma=False
    )
```

```python
import functools

import jax
import jax.numpy as jnp
from jax import lax
from jax.experimental import pallas as pl
from jax.experimental.pallas import tpu as pltpu
from jax.sharding import PartitionSpec as P

AXES = ("sx", "sy", "grp")
IN_VMEM = pl.BlockSpec(memory_space=pltpu.VMEM)
IN_PLACE = pl.BlockSpec(memory_space=pl.ANY)
PARAMS = pltpu.CompilerParams(vmem_limit_bytes=6 * 2**20)
LOADING = pltpu.CompilerParams(vmem_limit_bytes=9 * 2**20)
SHORT = pl.CostEstimate(flops=1, bytes_accessed=1, transcendentals=0)
LATE = 1
STAGES = 4
SHARES = (7, 9, 8)


def from_behind(block, axis, distance):
    devices = range(lax.axis_size(axis))
    route = [(i - distance, i) for i in devices if i - distance in devices]
    return lax.ppermute(block, axis, route)


def any_group(impedance, sources, match):
    zmatrix = impedance[0, 0]
    local_src = sources[0, 0].astype(jnp.float32)
    order = match[0, 0]
    total = zmatrix.shape[1]
    half = total // 2
    inverse = jnp.argsort(order)
    folded = jnp.take(zmatrix, inverse, axis=1)
    west_map = folded[:, :half]
    south_map = folded[:, half:]
    sweeps = lax.axis_size("sx") + lax.axis_size("sy") - 1
    outgoing = jnp.zeros(sources.shape[2:], jnp.bfloat16)
    for sweep_step in range(sweeps):
        whole = lax.all_gather(outgoing, "grp", axis=0, tiled=True)
        from_west = from_behind(whole[:half], "sx", 1)
        from_south = from_behind(whole[half:], "sy", 1)
        product = jnp.dot(west_map, from_west, preferred_element_type=jnp.float32)
        product = product + jnp.dot(south_map, from_south, preferred_element_type=jnp.float32)
        outgoing = (product + local_src).astype(jnp.bfloat16)
    return outgoing[None, None]


def routes(n_sx, n_sy, diagonal=None):
    number = lambda i, j, g: (i * n_sy + j) * 2 + g
    pairs = []
    for i in range(n_sx):
        for j in range(n_sy):
            if diagonal is not None and i + j != diagonal:
                continue
            if i + 1 < n_sx:
                pairs.append((number(i, j, 0), number(i + 1, j, 0)))
            if j + 1 < n_sy:
                pairs.append((number(i, j, 1), number(i, j + 1, 1)))
    return pairs


def is_active(step):
    diagonal = lax.axis_index("sx") + lax.axis_index("sy")
    if step == LATE:
        return (diagonal == step) | (diagonal == 0)
    return diagonal == step


def spans(half):
    unit = half // sum(SHARES)
    if half % sum(SHARES) or unit % 128:
        return [(0, half)]
    starts = [unit * sum(SHARES[:c]) for c in range(len(SHARES))]
    return [(at, unit * share) for at, share in zip(starts, SHARES)]


def block_of(extent, largest=512):
    return next(b for b in (largest, 256, 128, extent) if extent % b == 0)


def held(array):
    return pltpu.with_memory_space_constraint(array, pltpu.VMEM)


def load_kernel(pieces, zmap, *refs):
    stage, arrived = refs[-2:]
    slabs = refs[-2 - len(pieces):-2]
    depth, block, half = stage.shape
    count = zmap.shape[0] // block
    core = lax.axis_index("grp")

    side = core if pieces[0][0] else 1 - core

    def fetch(n):
        start = pl.multiple_of(side * half, 128)
        return pltpu.make_async_copy(
            zmap.at[pl.ds(n * block, block), pl.ds(start, half)], stage.at[n % depth], arrived.at[n % depth])

    for n in range(min(depth - 1, count)):
        fetch(n).start()
    for n in range(count):
        if n + depth - 1 < count:
            fetch(n + depth - 1).start()
        fetch(n).wait()
        for slab, (_, at, size) in zip(slabs, pieces):
            for k in range(0, size, 256):
                end = min(k + 256, size)
                slab[k:end, n * block:(n + 1) * block] = stage[n % depth, :, at + k:at + end].T


def load_call(zmap, pieces):
    rows, half = zmap.shape[0], zmap.shape[1] // 2
    return pl.pallas_call(
        functools.partial(load_kernel, pieces),
        out_shape=tuple(pltpu.VMEM((size, rows), zmap.dtype) for _, _, size in pieces),
        in_specs=[IN_PLACE], out_specs=tuple([IN_VMEM] * len(pieces)),
        scratch_shapes=[pltpu.VMEM((STAGES, block_of(rows, 256), half), zmap.dtype), pltpu.SemaphoreType.DMA((STAGES,))],
        compiler_params=LOADING, cost_estimate=pl.CostEstimate(
            flops=0, bytes_accessed=2 * rows * half, transcendentals=0),
    )(zmap)


def add_products(pieces, old, new):
    extent = new.shape[1]
    block = block_of(extent, 1024)
    flat = [(slab, trace[...].T) for slab, trace in pieces]
    for b in range(0, extent, block):
        total = None if old is None else old[:, b:b + block]
        for slab, trace in flat:
            term = jnp.dot(trace, slab[:, b:b + block], preferred_element_type=jnp.float32)
            total = term if total is None else total + term
        new[:, b:b + block] = total


def pick_rows(order, rows, out):
    count = out.shape[0]
    some = next(b for b in (128, 64, 32, 16, count) if count % b == 0)

    @pl.loop(0, count // some)
    def _(t):
        first = pl.multiple_of(t * some, some)
        picked = [rows[pl.ds(order[first + u], 1), :] for u in range(some)]
        out[pl.ds(first, some), :] = jnp.concatenate(picked, axis=0).astype(out.dtype)


def multiply_kernel(step, count, *refs):
    pieces = [(refs[2 * n], refs[2 * n + 1]) for n in range(count)]
    refs = refs[2 * count:]

    @pl.when(is_active(step))
    def _():
        add_products(pieces, refs[0] if len(refs) == 2 else None, refs[-1])


def finish_kernel(step, picks, slab, trace, acc, sources, *refs):
    if picks:
        order, _, rows, out, places, arrived = refs
        fetch = pltpu.make_async_copy(order, places, arrived)
    else:
        _, rows, out = refs

    @pl.when(is_active(step))
    def _():
        if picks:
            fetch.start()
        flat = trace[...].T
        extent = acc.shape[1]
        block = block_of(extent, 512)
        for b in range(0, extent, block):
            total = acc[:, b:b + block] + jnp.dot(
                flat, slab[:, b:b + block], preferred_element_type=jnp.float32)
            rows[b:b + block, :] = total.T + sources[b:b + block, :].astype(jnp.float32)
        if picks:
            fetch.wait()
            pick_rows(places, rows, out)

    if not picks:
        out[...] = rows[...].astype(out.dtype)


def pick_kernel(step, order, rows, out, places, arrived):
    @pl.when(is_active(step))
    def _():
        fetch = pltpu.make_async_copy(order, places, arrived)
        fetch.start()
        fetch.wait()
        pick_rows(places, rows, out)


def multiply_call(step, pieces, acc, rows, columns):
    args = [a for slab, trace in pieces for a in (held(slab), trace)]
    if acc is not None:
        args.append(held(acc))
    return pl.pallas_call(
        functools.partial(multiply_kernel, step, len(pieces)),
        out_shape=pltpu.VMEM((columns, rows), jnp.float32), in_specs=[IN_VMEM] * len(args), out_specs=IN_VMEM,
        input_output_aliases={} if acc is None else {len(args) - 1: 0}, compiler_params=PARAMS, cost_estimate=SHORT,
    )(*args)


def places_for(order):
    return [pltpu.SMEM(order.shape, order.dtype), pltpu.SemaphoreType.DMA]


def finish_call(step, slab, trace, acc, sources, order, rows):
    args = [held(slab), trace, held(acc), held(sources)]
    specs = [IN_VMEM] * 4
    if order is not None:
        args.append(order)
        specs.append(IN_PLACE)
        out = pltpu.VMEM((order.shape[0], rows.shape[1]), jnp.bfloat16)
    else:
        out = jax.ShapeDtypeStruct(rows.shape, jnp.bfloat16)
    args.append(held(rows))
    specs.append(IN_VMEM)
    return pl.pallas_call(
        functools.partial(finish_kernel, step, order is not None),
        out_shape=(pltpu.VMEM(rows.shape, rows.dtype), out), in_specs=specs, out_specs=(IN_VMEM, IN_VMEM),
        scratch_shapes=[] if order is None else places_for(order),
        input_output_aliases={len(args) - 1: 0}, compiler_params=PARAMS, cost_estimate=SHORT,
    )(*args)


def pick_call(step, order, rows):
    return pl.pallas_call(
        functools.partial(pick_kernel, step),
        out_shape=pltpu.VMEM((order.shape[0], rows.shape[1]), jnp.bfloat16),
        in_specs=[IN_PLACE, IN_VMEM], out_specs=IN_VMEM, scratch_shapes=places_for(order),
        compiler_params=PARAMS, cost_estimate=SHORT,
    )(order, held(rows))


def widen_kernel(source, rows):
    rows[...] = source[...].astype(rows.dtype)


def widen_call(source):
    return pl.pallas_call(
        widen_kernel, out_shape=pltpu.VMEM(source.shape, jnp.float32), in_specs=[IN_VMEM], out_specs=IN_VMEM,
        compiler_params=PARAMS, cost_estimate=SHORT,
    )(held(source))


def core_pair(impedance, sources, match):
    n_sx, n_sy = lax.axis_size("sx"), lax.axis_size("sy")
    core = lax.axis_index("grp")
    half = impedance.shape[3] // 2
    height, columns = sources.shape[2:]
    parts = spans(half)
    count = len(parts)
    source = sources[0, 0]

    wanted = lax.dynamic_slice(match[0, 0], (core * half,), (half,)) - core * half
    back = [(b, a) for a, b in routes(n_sx, n_sy)]
    order = lax.ppermute(wanted, AXES, back)
    orders = [order[at:at + size] for at, size in parts]

    zmap = impedance[0, 0]
    near = [(True, at, size) for at, size in parts]
    far = [(False, at, size) for at, size in parts]
    slabs = list(load_call(zmap, near))
    slabs, source = lax.optimization_barrier((slabs, source))
    rows = widen_call(source)
    sends = [pick_call(0, order, rows) for order in orders]
    zmap, sends = lax.optimization_barrier((zmap, sends))
    slabs = lax.optimization_barrier((*slabs, *load_call(zmap, far)))
    steps = n_sx + n_sy - 2
    for step in range(1, steps + 1):
        pairs = routes(n_sx, n_sy, step - 1)
        owns = [lax.ppermute(s, AXES, pairs) for s in sends]
        if step == 1:
            slabs, owns[0] = lax.optimization_barrier((slabs, owns[0]))
        acc, waiting = None, []
        for c, own in enumerate(owns):
            if c:
                acc, own = lax.optimization_barrier((acc, own))
            pieces = [(slabs[c], own)]
            pieces, waiting = pieces + waiting, []
            waiting.append((slabs[count + c], lax.ppermute(own, "grp", [(0, 1), (1, 0)])))
            acc = multiply_call(step, pieces, acc, height, columns)
        (slab, trace), = waiting
        if step == steps:
            rows, traces = finish_call(step, slab, trace, acc, source, None, rows)
        else:
            rows, first = finish_call(step, slab, trace, acc, source, orders[0], rows)
            sends = [first] + [pick_call(step, order, rows) for order in orders[1:]]
    return traces[None, None]


def solution(mesh):
    placed = (P("sx", "sy", "grp", None), P("sx", "sy", "grp", None), P("sx", "sy", None))
    body = core_pair if mesh.shape["grp"] == 2 else any_group
    return jax.shard_map(
        body, mesh=mesh, in_specs=placed, out_specs=P("sx", "sy", "grp", None), check_vma=False
    )
```

```python
import functools

import jax
import jax.numpy as jnp
from jax import lax
from jax.experimental import pallas as pl
from jax.experimental.pallas import tpu as pltpu
from jax.sharding import PartitionSpec as P

AXES = ("sx", "sy", "grp")
IN_VMEM = pl.BlockSpec(memory_space=pltpu.VMEM)
IN_PLACE = pl.BlockSpec(memory_space=pl.ANY)
PARAMS = pltpu.CompilerParams(vmem_limit_bytes=6 * 2**20)
LOADING = pltpu.CompilerParams(vmem_limit_bytes=9 * 2**20)
SHORT = pl.CostEstimate(flops=1, bytes_accessed=1, transcendentals=0)
LATE = 1
STAGES = 5
SHARES = (7, 9, 8)


def from_behind(block, axis, distance):
    devices = range(lax.axis_size(axis))
    route = [(i - distance, i) for i in devices if i - distance in devices]
    return lax.ppermute(block, axis, route)


def any_group(impedance, sources, match):
    zmatrix = impedance[0, 0]
    local_src = sources[0, 0].astype(jnp.float32)
    order = match[0, 0]
    total = zmatrix.shape[1]
    half = total // 2
    inverse = jnp.argsort(order)
    folded = jnp.take(zmatrix, inverse, axis=1)
    west_map = folded[:, :half]
    south_map = folded[:, half:]
    sweeps = lax.axis_size("sx") + lax.axis_size("sy") - 1
    outgoing = jnp.zeros(sources.shape[2:], jnp.bfloat16)
    for sweep_step in range(sweeps):
        whole = lax.all_gather(outgoing, "grp", axis=0, tiled=True)
        from_west = from_behind(whole[:half], "sx", 1)
        from_south = from_behind(whole[half:], "sy", 1)
        product = jnp.dot(west_map, from_west, preferred_element_type=jnp.float32)
        product = product + jnp.dot(south_map, from_south, preferred_element_type=jnp.float32)
        outgoing = (product + local_src).astype(jnp.bfloat16)
    return outgoing[None, None]


def routes(n_sx, n_sy, diagonal=None):
    number = lambda i, j, g: (i * n_sy + j) * 2 + g
    pairs = []
    for i in range(n_sx):
        for j in range(n_sy):
            if diagonal is not None and i + j != diagonal:
                continue
            if i + 1 < n_sx:
                pairs.append((number(i, j, 0), number(i + 1, j, 0)))
            if j + 1 < n_sy:
                pairs.append((number(i, j, 1), number(i, j + 1, 1)))
    return pairs


def is_active(step):
    diagonal = lax.axis_index("sx") + lax.axis_index("sy")
    if step == LATE:
        return (diagonal == step) | (diagonal == 0)
    return diagonal == step


def spans(half):
    unit = half // sum(SHARES)
    if half % sum(SHARES) or unit % 128:
        return [(0, half)]
    starts = [unit * sum(SHARES[:c]) for c in range(len(SHARES))]
    return [(at, unit * share) for at, share in zip(starts, SHARES)]


def block_of(extent, largest=512):
    return next(b for b in (largest, 256, 128, extent) if extent % b == 0)


def held(array):
    return pltpu.with_memory_space_constraint(array, pltpu.VMEM)


def load_kernel(pieces, zmap, *refs):
    stage, arrived = refs[-2:]
    slabs = refs[-2 - len(pieces):-2]
    depth, block, half = stage.shape
    count = zmap.shape[0] // block
    core = lax.axis_index("grp")

    side = core if pieces[0][0] else 1 - core

    def fetch(n):
        start = pl.multiple_of(side * half, 128)
        return pltpu.make_async_copy(
            zmap.at[pl.ds(n * block, block), pl.ds(start, half)], stage.at[n % depth], arrived.at[n % depth])

    for n in range(min(depth - 1, count)):
        fetch(n).start()
    for n in range(count):
        if n + depth - 1 < count:
            fetch(n + depth - 1).start()
        fetch(n).wait()
        for slab, (_, at, size) in zip(slabs, pieces):
            for k in range(0, size, 256):
                end = min(k + 256, size)
                slab[k:end, n * block:(n + 1) * block] = stage[n % depth, :, at + k:at + end].T


def load_call(zmap, pieces):
    rows, half = zmap.shape[0], zmap.shape[1] // 2
    return pl.pallas_call(
        functools.partial(load_kernel, pieces),
        out_shape=tuple(pltpu.VMEM((size, rows), zmap.dtype) for _, _, size in pieces),
        in_specs=[IN_PLACE], out_specs=tuple([IN_VMEM] * len(pieces)),
        scratch_shapes=[pltpu.VMEM((STAGES, block_of(rows, 256), half), zmap.dtype), pltpu.SemaphoreType.DMA((STAGES,))],
        compiler_params=LOADING, cost_estimate=pl.CostEstimate(
            flops=0, bytes_accessed=2 * rows * half, transcendentals=0),
    )(zmap)


def add_products(pieces, old, new):
    extent = new.shape[1]
    block = block_of(extent, 1024)
    flat = [(slab, trace[...].T) for slab, trace in pieces]
    for b in range(0, extent, block):
        total = None if old is None else old[:, b:b + block]
        for slab, trace in flat:
            term = jnp.dot(trace, slab[:, b:b + block], preferred_element_type=jnp.float32)
            total = term if total is None else total + term
        new[:, b:b + block] = total


def pick_rows(order, rows, out):
    count = out.shape[0]
    some = next(b for b in (128, 64, 32, 16, count) if count % b == 0)

    @pl.loop(0, count // some)
    def _(t):
        first = pl.multiple_of(t * some, some)
        picked = [rows[pl.ds(order[first + u], 1), :] for u in range(some)]
        out[pl.ds(first, some), :] = jnp.concatenate(picked, axis=0).astype(out.dtype)


def multiply_kernel(step, count, *refs):
    pieces = [(refs[2 * n], refs[2 * n + 1]) for n in range(count)]
    refs = refs[2 * count:]

    @pl.when(is_active(step))
    def _():
        add_products(pieces, refs[0] if len(refs) == 2 else None, refs[-1])


def finish_kernel(step, picks, slab, trace, acc, sources, *refs):
    if picks:
        order, _, rows, out, places, arrived = refs
        fetch = pltpu.make_async_copy(order, places, arrived)
    else:
        _, rows, out = refs

    @pl.when(is_active(step))
    def _():
        if picks:
            fetch.start()
        flat = trace[...].T
        extent = acc.shape[1]
        block = block_of(extent, 512)
        for b in range(0, extent, block):
            total = acc[:, b:b + block] + jnp.dot(
                flat, slab[:, b:b + block], preferred_element_type=jnp.float32)
            rows[b:b + block, :] = total.T + sources[b:b + block, :].astype(jnp.float32)
        if picks:
            fetch.wait()
            pick_rows(places, rows, out)

    if not picks:
        out[...] = rows[...].astype(out.dtype)


def pick_kernel(step, order, rows, out, places, arrived):
    @pl.when(is_active(step))
    def _():
        fetch = pltpu.make_async_copy(order, places, arrived)
        fetch.start()
        fetch.wait()
        pick_rows(places, rows, out)


def multiply_call(step, pieces, acc, rows, columns):
    args = [a for slab, trace in pieces for a in (held(slab), trace)]
    if acc is not None:
        args.append(held(acc))
    return pl.pallas_call(
        functools.partial(multiply_kernel, step, len(pieces)),
        out_shape=pltpu.VMEM((columns, rows), jnp.float32), in_specs=[IN_VMEM] * len(args), out_specs=IN_VMEM,
        input_output_aliases={} if acc is None else {len(args) - 1: 0}, compiler_params=PARAMS, cost_estimate=SHORT,
    )(*args)


def places_for(order):
    return [pltpu.SMEM(order.shape, order.dtype), pltpu.SemaphoreType.DMA]


def finish_call(step, slab, trace, acc, sources, order, rows):
    args = [held(slab), trace, held(acc), held(sources)]
    specs = [IN_VMEM] * 4
    if order is not None:
        args.append(order)
        specs.append(IN_PLACE)
        out = pltpu.VMEM((order.shape[0], rows.shape[1]), jnp.bfloat16)
    else:
        out = jax.ShapeDtypeStruct(rows.shape, jnp.bfloat16)
    args.append(held(rows))
    specs.append(IN_VMEM)
    return pl.pallas_call(
        functools.partial(finish_kernel, step, order is not None),
        out_shape=(pltpu.VMEM(rows.shape, rows.dtype), out), in_specs=specs, out_specs=(IN_VMEM, IN_VMEM),
        scratch_shapes=[] if order is None else places_for(order),
        input_output_aliases={len(args) - 1: 0}, compiler_params=PARAMS, cost_estimate=SHORT,
    )(*args)


def pick_call(step, order, rows):
    return pl.pallas_call(
        functools.partial(pick_kernel, step),
        out_shape=pltpu.VMEM((order.shape[0], rows.shape[1]), jnp.bfloat16),
        in_specs=[IN_PLACE, IN_VMEM], out_specs=IN_VMEM, scratch_shapes=places_for(order),
        compiler_params=PARAMS, cost_estimate=SHORT,
    )(order, held(rows))


def widen_kernel(source, rows):
    rows[...] = source[...].astype(rows.dtype)


def widen_call(source):
    return pl.pallas_call(
        widen_kernel, out_shape=pltpu.VMEM(source.shape, jnp.float32), in_specs=[IN_VMEM], out_specs=IN_VMEM,
        compiler_params=PARAMS, cost_estimate=SHORT,
    )(held(source))


def core_pair(impedance, sources, match):
    n_sx, n_sy = lax.axis_size("sx"), lax.axis_size("sy")
    core = lax.axis_index("grp")
    half = impedance.shape[3] // 2
    height, columns = sources.shape[2:]
    parts = spans(half)
    count = len(parts)
    source = sources[0, 0]

    wanted = lax.dynamic_slice(match[0, 0], (core * half,), (half,)) - core * half
    back = [(b, a) for a, b in routes(n_sx, n_sy)]
    order = lax.ppermute(wanted, AXES, back)
    orders = [order[at:at + size] for at, size in parts]

    zmap = impedance[0, 0]
    near = [(True, at, size) for at, size in parts]
    far = [(False, at, size) for at, size in parts]
    slabs = list(load_call(zmap, near))
    slabs, source = lax.optimization_barrier((slabs, source))
    rows = widen_call(source)
    sends = [pick_call(0, order, rows) for order in orders]
    zmap, sends = lax.optimization_barrier((zmap, sends))
    slabs = lax.optimization_barrier((*slabs, *load_call(zmap, far)))
    steps = n_sx + n_sy - 2
    for step in range(1, steps + 1):
        pairs = routes(n_sx, n_sy, step - 1)
        owns = [lax.ppermute(s, AXES, pairs) for s in sends]
        if step == 1:
            slabs, owns[0] = lax.optimization_barrier((slabs, owns[0]))
        acc, waiting = None, []
        for c, own in enumerate(owns):
            if c:
                acc, own = lax.optimization_barrier((acc, own))
            pieces = [(slabs[c], own)]
            pieces, waiting = pieces + waiting, []
            waiting.append((slabs[count + c], lax.ppermute(own, "grp", [(0, 1), (1, 0)])))
            acc = multiply_call(step, pieces, acc, height, columns)
        (slab, trace), = waiting
        if step == steps:
            rows, traces = finish_call(step, slab, trace, acc, source, None, rows)
        else:
            rows, first = finish_call(step, slab, trace, acc, source, orders[0], rows)
            sends = [first] + [pick_call(step, order, rows) for order in orders[1:]]
    return traces[None, None]


def solution(mesh):
    placed = (P("sx", "sy", "grp", None), P("sx", "sy", "grp", None), P("sx", "sy", None))
    body = core_pair if mesh.shape["grp"] == 2 else any_group
    return jax.shard_map(
        body, mesh=mesh, in_specs=placed, out_specs=P("sx", "sy", "grp", None), check_vma=False
    )
```
